32 devices in a mesh: groups: 2 (over x), expert: 4 (over y, core), inner: 4 (over z).
Axes of the slice: x: 2, y: 2, z: 4, core: 2. Of those that a mesh axis runs over, the one named last changes fastest.
Arguments:
- quant_rows: bfloat16 [256, 7168], P(('groups', 'expert', 'inner')), parts along dimension 0, may hold values from -4 to 4
- block_scales: bfloat16 [256, 56], P(('groups', 'expert', 'inner')), parts along dimension 0, may hold values from 0.29882812 to 3
- expert_ids: int32 [256, 2], P(('groups', 'expert', 'inner')), parts along dimension 0, may hold values from 0 to 3, all different within a row; in each aligned block of 8 rows (0 to 7, 8 to 15, ...) at most 5 rows name the same one
- gate_scores: float32 [256, 2], P(('groups', 'expert', 'inner')), parts along dimension 0, may hold values from 0.005 to 1
- w_gate: bfloat16 [4, 7168, 2048], P('expert', None, 'inner'), may hold values from -0.0625 to 0.0625
- w_up: bfloat16 [4, 7168, 2048], P('expert', None, 'inner'), may hold values from -0.0625 to 0.0625
- w_down: bfloat16 [4, 2048, 7168], P('expert', 'inner'), may hold values from -0.125 to 0.125
- sketch: bfloat16 [4, 7168, 256], P('expert', 'inner'), may hold values from -0.0625 to 0.0625
- owner_map: int32 [4], replicated, may hold values from 0 to 15, as said below
Outputs:
- mixed: bfloat16 [256, 7168], P(('groups', 'expert', 'inner')), parts along dimension 0
- gram: float32 [32, 256, 256], P(('groups', 'expert', 'inner')), parts along dimension 0
The draws below stay inside these ranges and needn't reach their ends.
There are 2 independent parts, one for each index of `groups`. The reference program is written for one: setup_inputs(seed, part) draws one part's arguments, and reference() takes and returns one part's arrays. A program takes and returns all parts, laid end to end along the dimension named above; an argument that names none is the same for every part. Nothing has to cross between parts.
Inputs may be any that keep to these rules, and one draw needn't show every extreme that they name: `expert_ids`: each token names 2 different experts; in each aligned block of 8 tokens no expert is named by more than 5 tokens, and in every draw some block has an expert named by exactly 5 tokens. `owner_map`: in every draw some expert e has its owner in the group of owners e + 4 // 2 (counted round), groups being 4 consecutive owners.
All inputs are finite; a program needn't handle non-finite values.
Results may differ from the reference program's by a relative error of at most 0.014.
Values may be sent and summed in bfloat16 or wider, within the bound.
A program may use at most 192 MiB of HBM per device.

```python
import math
import jax
import jax.numpy as jnp
import numpy as np
from jax import lax

D = 7168
FF = 2048
SK = 256
BLK = 128
TOK_DEV = 8
EXPERTS = 4
TOP = 2
CAP = 5
OWNERS = 16
TOKENS = 128
HID_BLK = 512


def draw_owner_map(key, part):
    key = jax.random.fold_in(key, 7)
    key_offset, key_far, key_inner = jax.random.split(key, 3)
    group_size = OWNERS // EXPERTS
    positions = jnp.arange(EXPERTS, dtype=jnp.int32)
    offsets = jax.random.randint(key_offset, (EXPERTS,), 0, EXPERTS, dtype=jnp.int32)
    far_expert = jax.random.randint(key_far, (), 0, EXPERTS, dtype=jnp.int32)
    offsets = jnp.where(positions == far_expert, EXPERTS // 2, offsets)
    inner_pick = jax.random.randint(key_inner, (EXPERTS,), 0, group_size, dtype=jnp.int32)
    return ((positions + offsets) % EXPERTS * group_size + inner_pick).astype(jnp.int32)


def levels(own_key, dims, cuts, low, high):
    loudness, own = 1.0, jax.random.fold_in(own_key, 6)
    for position, shards_of in cuts:
        draws = jnp.exp(jax.random.uniform(jax.random.fold_in(own, position), (shards_of,), jnp.float32, low / len(cuts), high / len(cuts)))
        loudness = loudness * jnp.repeat(draws, dims[position] // shards_of).reshape([-1 if axis == position else 1 for axis in range(len(dims))])
    return loudness


def routed_block(key, own, number, rows, number_of, top, most, skew):
    sequence = jax.random.permutation(key, number_of)
    heavy_load, usual = shares(number_of, rows * top, most, skew, True), shares(number_of, rows * top, most, skew, False)
    places = jnp.arange(number_of)

    def named(sizes, offset_by):
        used = int((sizes > 0).sum())
        fixed = max(1, used // 4)
        moved = fixed + (places - fixed + offset_by * (used - fixed)) % max(1, number_of - fixed)
        return jnp.zeros((number_of,), jnp.int32).at[sequence[jnp.where(places < fixed, places, moved)]].set(jnp.asarray(sizes, jnp.int32))

    sizes = jnp.where(number % 4 == 0, named(heavy_load, number // 4), named(usual, number - number // 4 - 1))
    mixed = jax.random.permutation(jax.random.fold_in(own, 3), number_of)
    donor, taker = mixed[0:number_of // 2 * 2:2], mixed[1:number_of // 2 * 2:2]
    margin = jnp.minimum(sizes[donor] - 1, most - sizes[taker]) // 2
    margin = jnp.where((donor == sequence[0]) | (taker == sequence[0]) | (sizes[taker] == 0), 0, jnp.maximum(margin, 0))
    moved = jax.random.randint(jax.random.fold_in(own, 4), (number_of // 2,), 0, 1 << 20) % (margin + 1)
    sizes = sizes.at[donor].add(-moved).at[taker].add(moved)
    labels = jnp.searchsorted(jnp.cumsum(sizes), jnp.arange(rows * top), side="right").astype(jnp.int32)
    table = labels.reshape(top, rows).T
    table = table[jax.random.permutation(jax.random.fold_in(own, 1), rows)]
    offset_by = jax.random.randint(jax.random.fold_in(own, 2), (rows, 1), 0, top)
    return jnp.take_along_axis(table, (jnp.arange(top)[None, :] + offset_by) % top, axis=1)


def shares(count, total, most, slope, full):
    loads = [(1 << 20) // math.isqrt(standing ** slope) + 1 for standing in range(1, count + 1)]
    largest = most if full else min(most, max(-(-total // count), total * loads[0] // sum(loads)))
    least = 1 if total - largest >= count - 1 else 0
    counts, rest = [largest] + [least] * (count - 1), total - largest - least * (count - 1)
    while rest > 0:
        candidates = [i for i in range(1, count) if counts[i] < largest] or [i for i in range(1, count) if counts[i] < most]
        whole, remaining = sum([loads[i] for i in candidates]), rest
        for i in candidates:
            more = min(most - counts[i], max(1, remaining * loads[i] // whole), rest)
            counts[i] = counts[i] + more
            rest = rest - more
    return np.array(counts)


def gaussian(stream_key, extent, deviation, reach, cuts=(), kind=jnp.bfloat16):
    entries = jax.random.normal(stream_key, extent, jnp.float32) * deviation
    if len(cuts) > 0:
        entries = levels(stream_key, extent, cuts, -0.22, 0.18) * entries
    return jnp.clip(entries, min=-reach, max=reach).astype(kind)


def setup_inputs(seed: int = 0, part: int = 0) -> dict:
    seeds = jax.random.split(jax.random.key(seed), 10)
    own_keys = jax.random.split(jax.random.fold_in(seeds[9], part), 10)
    quant_rows = gaussian(own_keys[0], (TOKENS, D), 1.0, 4.0, ((0, 16),))
    block_scales = jnp.clip(jnp.exp(math.log(3.0) - 2.306499 * jax.random.uniform(own_keys[1], (TOKENS, D // BLK), jnp.float32) ** levels(own_keys[1], (TOKENS, D // BLK), ((0, 16),), -0.2, 0.2)), 0.29882812, 3.0).astype(jnp.bfloat16)
    expert_ids_keys = jax.random.split(jax.random.fold_in(own_keys[2], 1), TOKENS // TOK_DEV)
    expert_ids_turns = jax.random.permutation(jax.random.fold_in(own_keys[2], 3), TOKENS // TOK_DEV)
    expert_ids = jax.vmap(lambda own, number: routed_block(jax.random.fold_in(own_keys[2], 2), own, number, TOK_DEV, EXPERTS, TOP, CAP, 1))(expert_ids_keys, expert_ids_turns).reshape((TOKENS, TOP))
    gate_scores = jnp.clip(jnp.exp(math.log(1.0) - 5.2983174 * jax.random.uniform(own_keys[3], (TOKENS, TOP), jnp.float32) ** levels(own_keys[3], (TOKENS, TOP), ((0, 16),), -0.2, 0.2)), 0.005, 1.0)
    w_gate = gaussian(seeds[4], (EXPERTS, D, FF), D ** -0.5, 0.0625, ((0, 4), (2, 4)))
    w_up = gaussian(seeds[5], (EXPERTS, D, FF), D ** -0.5, 0.0625, ((0, 4), (2, 4)))
    w_down = gaussian(seeds[6], (EXPERTS, FF, D), FF ** -0.5, 0.125, ((0, 4), (1, 4)))
    sketch = gaussian(seeds[7], (EXPERTS, D, SK), D ** -0.5, 0.0625, ((0, 4), (1, 4)))
    owner_map = draw_owner_map(jax.random.fold_in(seeds[9], 71), part)
    return {"quant_rows": quant_rows, "block_scales": block_scales, "expert_ids": expert_ids, "gate_scores": gate_scores, "w_gate": w_gate, "w_up": w_up, "w_down": w_down, "sketch": sketch, "owner_map": owner_map}


def expert_pass(padded, block_table, gate_w, up_w, down_w, sketch_w):
    expert_in = padded[block_table.reshape(-1)]
    gate_proj = jnp.dot(expert_in, gate_w, preferred_element_type=jnp.float32)
    up_proj = jnp.dot(expert_in, up_w, preferred_element_type=jnp.float32)
    hidden = (jax.nn.silu(gate_proj) * up_proj).astype(jnp.bfloat16)
    summed = jnp.zeros((expert_in.shape[0], D), jnp.float32)
    for block_idx in range(FF // HID_BLK):
        lower = block_idx * HID_BLK
        part_sum = jnp.dot(hidden[:, lower:lower + HID_BLK], down_w[lower:lower + HID_BLK],
                           preferred_element_type=jnp.float32).astype(jnp.bfloat16)
        summed = summed + lax.optimization_barrier(part_sum).astype(jnp.float32)
    expert_out = summed.astype(jnp.bfloat16)
    sketched = jnp.dot(expert_in, sketch_w, preferred_element_type=jnp.float32)
    gram_part = jnp.dot(sketched.T, sketched, precision=lax.Precision.HIGHEST) / TOKENS
    return expert_out, gram_part


def reference(quant_rows, block_scales, expert_ids, gate_scores, w_gate, w_up, w_down, sketch, owner_map):
    blocks = TOKENS // TOK_DEV
    expanded = quant_rows.astype(jnp.float32).reshape(TOKENS, D // BLK, BLK) * block_scales.astype(jnp.float32)[:, :, None]
    dequant = expanded.reshape(TOKENS, D).astype(jnp.bfloat16)
    route_ids = expert_ids.reshape(blocks, TOK_DEV * TOP)
    onehot = (route_ids[:, :, None] == jnp.arange(EXPERTS, dtype=jnp.int32)[None, None, :]).astype(jnp.int32)
    slot_rank = jnp.sum((jnp.cumsum(onehot, axis=1) - onehot) * onehot, axis=2).astype(jnp.int32)
    source_token = (jnp.arange(blocks * TOK_DEV * TOP, dtype=jnp.int32) // TOP).reshape(blocks, TOK_DEV * TOP)
    block_index = jnp.broadcast_to(jnp.arange(blocks, dtype=jnp.int32)[:, None], route_ids.shape)
    slot_table = jnp.full((EXPERTS, blocks, CAP), TOKENS, jnp.int32)
    slot_table = slot_table.at[route_ids, block_index, slot_rank].set(source_token)
    padded = jnp.concatenate([dequant, jnp.zeros((1, D), jnp.bfloat16)], axis=0)

    def one_expert(pieces):
        return expert_pass(padded, pieces[0], pieces[1], pieces[2], pieces[3], pieces[4])

    expert_out, gram_parts = lax.map(one_expert, (slot_table, w_gate, w_up, w_down, sketch))
    flat_rows = (block_index * CAP + slot_rank).reshape(-1)
    picked = expert_out[route_ids.reshape(-1), flat_rows].astype(jnp.float32).reshape(TOKENS, TOP, D)
    weights = 2.5 * gate_scores / jnp.sum(gate_scores, axis=1, keepdims=True)
    mixed = jnp.sum(picked * weights[:, :, None], axis=1).astype(jnp.bfloat16)
    chosen = (owner_map[None, :] == jnp.arange(OWNERS, dtype=jnp.int32)[:, None]).astype(jnp.float32)
    gram = jnp.dot(chosen, gram_parts.reshape(EXPERTS, SK * SK),
                   precision=lax.Precision.HIGHEST).reshape(OWNERS, SK, SK)
    return mixed, gram
```

```python
import functools

import jax
import jax.numpy as jnp
from jax import lax
from jax.experimental import pallas as pl
from jax.experimental.pallas import tpu as pltpu
from jax.sharding import PartitionSpec as P

CAP = 5
BLOCKS = 2
LANES = 128
MESH = pl.DeviceIdType.MESH


def exchange_plan(
    quant_rows, block_scales, expert_ids, gate_scores, w_gate, w_up, w_down, sketch, owner_map
):
    n_expert = lax.axis_size("expert")
    n_inner = lax.axis_size("inner")
    all_blocks = n_expert * n_inner
    tok_count, top_count = expert_ids.shape
    model_width = quant_rows.shape[1]
    scale_cols = block_scales.shape[1]
    experts = owner_map.shape[0]
    sketch_cols = sketch.shape[2]
    total_rows = all_blocks * CAP
    flat_ids = expert_ids.reshape(-1)
    onehot = (flat_ids[:, None] == jnp.arange(experts, dtype=jnp.int32)[None, :]).astype(jnp.int32)
    slot_rank = jnp.sum((jnp.cumsum(onehot, axis=0) - onehot) * onehot, axis=1)
    source_token = jnp.arange(tok_count * top_count, dtype=jnp.int32) // top_count
    slot_table = (
        jnp.full((experts * CAP,), tok_count, jnp.int32)
        .at[flat_ids * CAP + slot_rank]
        .set(source_token)
    )
    padded_rows = jnp.concatenate([quant_rows, jnp.zeros((1, model_width), jnp.bfloat16)], axis=0)
    padded_scales = jnp.concatenate(
        [block_scales, jnp.zeros((1, scale_cols), jnp.bfloat16)], axis=0
    )
    send_rows = padded_rows[slot_table].reshape(experts, CAP, model_width)
    send_scales = padded_scales[slot_table].reshape(experts, CAP, scale_cols)
    wide_rows = jnp.broadcast_to(send_rows[:, None], (experts, n_inner, CAP, model_width))
    wide_scales = jnp.broadcast_to(send_scales[:, None], (experts, n_inner, CAP, scale_cols))
    inner_rows, inner_scales = (
        lax.all_to_all(
            wide_rows.reshape(all_blocks, CAP, model_width),
            ("expert", "inner"),
            split_axis=0,
            concat_axis=0,
            tiled=True,
        ),
        lax.all_to_all(
            wide_scales.reshape(all_blocks, CAP, scale_cols),
            ("expert", "inner"),
            split_axis=0,
            concat_axis=0,
            tiled=True,
        ),
    )
    expanded = inner_rows.reshape(total_rows, scale_cols, model_width // scale_cols).astype(
        jnp.float32
    )
    expanded = expanded * inner_scales.reshape(total_rows, scale_cols, 1).astype(jnp.float32)
    dequant = expanded.reshape(total_rows, model_width).astype(jnp.bfloat16)
    gate_w = w_gate[0]
    up_w = w_up[0]
    down_w = w_down[0]
    gate_proj = jnp.dot(dequant, gate_w, preferred_element_type=jnp.float32)
    up_proj = jnp.dot(dequant, up_w, preferred_element_type=jnp.float32)
    hidden = (jax.nn.silu(gate_proj) * up_proj).astype(jnp.bfloat16)
    partial_value = (
        jnp.dot(hidden, down_w, preferred_element_type=jnp.float32)
        .astype(jnp.bfloat16)
        .reshape(all_blocks, CAP, model_width)
    )
    returned = lax.all_to_all(
        partial_value, ("expert", "inner"), split_axis=0, concat_axis=0, tiled=True
    )
    returned = returned.reshape(n_expert, n_inner, CAP, model_width).astype(jnp.float32)
    outputs = jnp.sum(returned, axis=1).astype(jnp.bfloat16)
    picked = (
        outputs[flat_ids, slot_rank].reshape(tok_count, top_count, model_width).astype(jnp.float32)
    )
    totals = jnp.sum(gate_scores, axis=1, keepdims=True)
    weights = 2.5 * gate_scores / totals
    mixed = jnp.sum(picked * weights[:, :, None], axis=1).astype(jnp.bfloat16)
    part_rows = sketch.shape[1]
    first_col = lax.axis_index("inner") * part_rows
    column_part = lax.dynamic_slice_in_dim(dequant, first_col, part_rows, 1)
    sketched = lax.psum(
        jnp.dot(column_part, sketch[0], preferred_element_type=jnp.float32).astype(jnp.bfloat16),
        "inner",
    ).astype(jnp.float32)
    gram_local = jnp.dot(sketched.T, sketched, precision=lax.Precision.HIGHEST) / (
        tok_count * all_blocks
    )
    gram_all = lax.all_gather(
        gram_local[None].astype(jnp.bfloat16), "expert", axis=0, tiled=True
    ).astype(jnp.float32)
    own_rank = lax.axis_index("expert") * n_inner + lax.axis_index("inner")
    chosen = (owner_map == own_rank).astype(jnp.float32)
    gram_out = jnp.dot(
        chosen[None, :],
        gram_all.reshape(experts, sketch_cols * sketch_cols),
        precision=lax.Precision.HIGHEST,
    ).reshape(1, sketch_cols, sketch_cols)
    return (mixed, gram_out)


def layer_kernel(
    n_inner,
    experts,
    quant_ref,
    scale_ref,
    ids_ref,
    score_ref,
    gate_hbm,
    up_hbm,
    down_hbm,
    sketch_hbm,
    owner_ref,
    mixed_ref,
    gram_ref,
    gate_w,
    up_w,
    down_w,
    sketch_w,
    swap_out,
    swap_in,
    rows,
    sk_part,
    sk_in,
    sk_all,
    hidden,
    own_part,
    sib_out,
    sib_in,
    y_out,
    y_in,
    up_out,
    up_in,
    dn_out,
    dn_in,
    last,
    last_in,
    load_sem,
    swap_sem,
    zup_s,
    zup_r,
    zdn_s,
    zdn_r,
    yg_s,
    yg_r,
    sg_s,
    sg_r,
    skx_s,
    skx_r,
    ska_s,
    ska_r,
    sib_s,
    sib_r,
    yr_s,
    yr_r,
    ur_s,
    ur_r,
    dr_s,
    dr_r,
    last_sem,
):
    expert = lax.axis_index("expert")
    z = lax.axis_index("inner")
    y, c = expert // 2, expert % 2
    sibling = {"expert": y * 2 + (1 - c), "inner": z}
    y_peer = {"expert": (1 - y) * 2 + c, "inner": z}
    above = {"expert": expert, "inner": lax.rem(z + 1, n_inner)}
    below = {"expert": expert, "inner": lax.rem(z + n_inner - 1, n_inner)}
    n_expert = 4
    devices = n_expert * n_inner
    chunks = 2 * n_inner
    tok = quant_ref.shape[0]
    width = quant_ref.shape[1]
    half = width // 2
    blk = width // scale_ref.shape[1]
    total = chunks * 2 * tok
    rank = expert * n_inner + z

    def send(src, dst, send_sem, recv_sem, device):
        return pltpu.make_async_remote_copy(
            src_ref=src,
            dst_ref=dst,
            send_sem=send_sem,
            recv_sem=recv_sem,
            device_id=device,
            device_id_type=MESH,
        )

    loads = [
        pltpu.make_async_copy(sketch_hbm.at[0], sketch_w, load_sem.at[0]),
        pltpu.make_async_copy(gate_hbm.at[0], gate_w, load_sem.at[1]),
        pltpu.make_async_copy(up_hbm.at[0], up_w, load_sem.at[2]),
        pltpu.make_async_copy(down_hbm.at[0], down_w, load_sem.at[3]),
    ]

    barrier = pltpu.get_barrier_semaphore()
    for step in range(1, devices):
        other = lax.rem(rank + step, devices)
        pl.semaphore_signal(
            barrier,
            inc=1,
            device_id={"expert": other // n_inner, "inner": lax.rem(other, n_inner)},
            device_id_type=MESH,
        )
    for load in loads:
        load.start()

    quant = quant_ref[...].astype(jnp.float32)
    scales = scale_ref[...].astype(jnp.float32)
    for j in range(width // blk):
        part = quant[:, j * blk : (j + 1) * blk] * scales[:, j : j + 1]
        h, col = divmod(j * blk, half)
        swap_out[h, :, col : col + blk] = part.astype(jnp.bfloat16).astype(jnp.float32)
    ids = ids_ref[...]
    scores = score_ref[...]
    weights = 2.5 * scores / jnp.sum(scores, axis=1, keepdims=True)
    lane = lax.broadcasted_iota(jnp.int32, (tok, LANES), 1)
    meta = jnp.zeros((tok, LANES), jnp.float32)
    for k in range(ids.shape[1]):
        named = ids[:, k : k + 1]
        value = weights[:, k : k + 1]
        high = value.astype(jnp.bfloat16).astype(jnp.float32)
        meta = jnp.where(lane == named, high, meta)
        meta = jnp.where(lane == named + experts, value - high, meta)
        meta = jnp.where(lane == named + 2 * experts, 1.0, meta)
    for h in range(2):
        swap_out[h, :, half:] = meta

    pl.semaphore_wait(barrier, devices - 1)

    swap = send(swap_out.at[1 - c], swap_in, swap_sem.at[0], swap_sem.at[1], sibling)
    swap.start()
    swap.wait()
    mine = y * n_inner + z

    @pl.when(c == 0)
    def _():
        rows[0, mine] = jnp.concatenate([swap_out[0], swap_in[...]], axis=0).astype(jnp.bfloat16)

    @pl.when(c == 1)
    def _():
        rows[1, mine] = jnp.concatenate([swap_in[...], swap_out[1]], axis=0).astype(jnp.bfloat16)

    def gather_up(src):
        ref = rows.at[c, y * n_inner + src]
        return send(ref, ref, zup_s.at[src], zup_r.at[src], above)

    def gather_dn(src):
        ref = rows.at[c, y * n_inner + src]
        return send(ref, ref, zdn_s.at[src], zdn_r.at[src], below)

    def gather_y(src):
        ref = rows.at[c, y * n_inner + src]
        return send(ref, ref, yg_s.at[src], yg_r.at[src], y_peer)

    def from_y(src):
        ref = rows.at[c, (1 - y) * n_inner + src]
        return send(ref, ref, yg_s.at[src], yg_r.at[src], y_peer)

    def gather_sib(chunk):
        ref = rows.at[c, chunk]
        return send(ref, ref, sg_s.at[chunk], sg_r.at[chunk], sibling)

    def from_sib(chunk):
        ref = rows.at[1 - c, chunk]
        return send(ref, ref, sg_s.at[chunk], sg_r.at[chunk], sibling)

    def when_y(src):
        from_y(src).wait_recv()
        gather_sib((1 - y) * n_inner + src).start()

    @pl.when(z < n_inner - 1)
    def _():
        gather_up(z).start()

    @pl.when(z > 0)
    def _():
        gather_dn(z).start()

    gather_y(z).start()
    gather_sib(mine).start()
    for s in range(1, n_inner):

        @pl.when(z - s >= 0)
        def _():
            src = lax.rem(z - s + n_inner, n_inner)
            gather_up(src).wait_recv()

            @pl.when(z < n_inner - 1)
            def _():
                gather_up(src).start()

            gather_y(src).start()
            gather_sib(y * n_inner + src).start()

        @pl.when(z + s < n_inner)
        def _():
            src = lax.rem(z + s, n_inner)
            gather_dn(src).wait_recv()

            @pl.when(z > 0)
            def _():
                gather_dn(src).start()

            gather_y(src).start()
            gather_sib(y * n_inner + src).start()

        if s == 1:
            when_y(z)
        else:

            @pl.when(z - s + 1 >= 0)
            def _():
                when_y(lax.rem(z - s + 1 + n_inner, n_inner))

            @pl.when(z + s - 1 < n_inner)
            def _():
                when_y(lax.rem(z + s - 1, n_inner))

    s = n_inner - 1

    @pl.when(z - s >= 0)
    def _():
        when_y(lax.rem(z - s + n_inner, n_inner))

    @pl.when(z + s < n_inner)
    def _():
        when_y(lax.rem(z + s, n_inner))

    for chunk in range(chunks):
        from_sib(chunk).wait_recv()

    info = rows[0, :, :, half:].reshape(total, LANES).astype(jnp.float32)
    lanes = lax.broadcasted_iota(jnp.int32, (total, LANES), 1)

    def column(index):
        return jnp.sum(jnp.where(lanes == index, info, 0.0), axis=1, keepdims=True)

    weight = column(expert) + column(expert + experts)
    routed = column(expert + 2 * experts)

    share = sketch_w.shape[0]
    per_half = half // share
    loads[0].wait()
    start = pl.multiple_of(lax.rem(z, per_half) * share, LANES)
    columns = rows[z // per_half, :, :, pl.ds(start, share)].reshape(total, share)
    product = jnp.dot(columns, sketch_w[...], preferred_element_type=jnp.float32) * routed
    cols = product.shape[1]
    group = total // n_inner
    sk_part[...] = product.astype(jnp.bfloat16).reshape(n_inner, group, cols)

    def sk_exchange(step):
        to = lax.rem(z + step, n_inner)
        return send(
            sk_part.at[to],
            sk_in.at[step],
            skx_s.at[step],
            skx_r.at[step],
            {"expert": expert, "inner": to},
        )

    for step in range(1, n_inner):
        sk_exchange(step).start()

    x0 = rows[0, :, :, :half].reshape(total, half)
    x1 = rows[1, :, :, :half].reshape(total, half)
    loads[1].wait()
    loads[2].wait()
    tile = 256

    def project(n):
        at = slice(n * tile, (n + 1) * tile)
        gate = jnp.dot(x0, gate_w[:half, at], preferred_element_type=jnp.float32)
        gate += jnp.dot(x1, gate_w[half:, at], preferred_element_type=jnp.float32)
        up = jnp.dot(x0, up_w[:half, at], preferred_element_type=jnp.float32)
        up += jnp.dot(x1, up_w[half:, at], preferred_element_type=jnp.float32)
        hidden[:, at] = (gate / (1.0 + jnp.exp(-gate)) * up).astype(jnp.bfloat16)

    tiles = hidden.shape[1] // tile
    project(0)

    summed = sk_part[z].astype(jnp.float32)
    for step in range(1, n_inner):
        sk_exchange(step).wait()
        summed += sk_in[step].astype(jnp.float32)
    sk_all[rank] = summed.astype(jnp.bfloat16)

    def sk_gather(step):
        to = lax.rem(rank + step, devices)
        return send(
            sk_all.at[rank],
            sk_all.at[rank],
            ska_s.at[step],
            ska_r.at[step],
            {"expert": to // n_inner, "inner": lax.rem(to, n_inner)},
        )

    def sk_arrival(step):
        origin = lax.rem(rank - step + devices, devices)
        return send(
            sk_all.at[origin], sk_all.at[origin], ska_s.at[step], ska_r.at[step], sibling
        )

    for step in range(1, devices):
        sk_gather(step).start()

    for n in range(1, tiles):
        project(n)

    loads[3].wait()
    blocks, _, _, wide = own_part.shape

    def down(h, b):
        at = pl.ds(pl.multiple_of(h * half + b * wide, LANES), wide)
        out = jnp.dot(hidden[...], down_w[:, at], preferred_element_type=jnp.float32)
        return (out * weight).reshape(chunks, 2 * tok, wide)

    def to_sib(b):
        return send(sib_out.at[b], sib_in.at[b], sib_s.at[b], sib_r.at[b], sibling)

    def reduce_y(b, dest):
        return send(y_out.at[b, dest], y_in.at[b, dest], yr_s.at[b, dest], yr_r.at[b, dest], y_peer)

    def reduce_up(b, dest):
        return send(up_out.at[b, dest], up_in.at[b, dest], ur_s.at[b, dest], ur_r.at[b, dest], above)

    def reduce_dn(b, dest):
        return send(dn_out.at[b, dest], dn_in.at[b, dest], dr_s.at[b, dest], dr_r.at[b, dest], below)

    def chip_sum(b, y_to, dest):
        at = y_to * n_inner + dest
        return own_part[b, at] + sib_in[b, at].astype(jnp.float32)

    order = []
    for i in range(n_inner // 2):
        order += [n_inner - 1 - i, i]

    def start_y(b):
        to_sib(b).wait_recv()
        for dest in order:
            y_out[b, dest] = chip_sum(b, 1 - y, dest).astype(jnp.bfloat16)
            reduce_y(b, dest).start()

    for b in range(blocks):
        sib_out[b] = down(1 - c, b).astype(jnp.bfloat16)
        to_sib(b).start()
        own_part[b] = down(c, b)
        start_y(b)

    def add_y(b, dest):
        reduce_y(b, dest).wait_recv()
        own_part[b, y * n_inner + dest] = chip_sum(b, y, dest) + y_in[b, dest].astype(jnp.float32)

    arrived = set()
    for i in range(n_inner - 1):
        for b in range(blocks):
            top, low = n_inner - 1 - i, i
            for dest in (top, low):
                if (b, dest) not in arrived:
                    arrived.add((b, dest))
                    add_y(b, dest)

            @pl.when(z < top)
            def _():
                up_out[b, top] = own_part[b, y * n_inner + top].astype(jnp.bfloat16)

                @pl.when(z > 0)
                def _():
                    reduce_up(b, top).wait_recv()
                    up_out[b, top] = (
                        own_part[b, y * n_inner + top] + up_in[b, top].astype(jnp.float32)
                    ).astype(jnp.bfloat16)

                reduce_up(b, top).start()

            @pl.when(z > low)
            def _():
                dn_out[b, low] = own_part[b, y * n_inner + low].astype(jnp.bfloat16)

                @pl.when(z < n_inner - 1)
                def _():
                    reduce_dn(b, low).wait_recv()
                    dn_out[b, low] = (
                        own_part[b, y * n_inner + low] + dn_in[b, low].astype(jnp.float32)
                    ).astype(jnp.bfloat16)

                reduce_dn(b, low).start()

    for step in range(1, devices):
        sk_arrival(step).wait_recv()
    gram = jnp.zeros((cols, cols), jnp.float32)
    for e in range(experts):
        chosen = jnp.where(owner_ref[e] == rank, 1.0 / total, 0.0).astype(jnp.float32)
        part = sk_all[e * n_inner : (e + 1) * n_inner].reshape(total, cols)
        gram += chosen * lax.dot_general(
            part, part, (((0,), (0,)), ((), ())), preferred_element_type=jnp.float32
        )
    gram_ref[0] = gram

    for b in range(blocks):

        @pl.when(z > 0)
        def _():
            reduce_up(b, z).wait_recv()
            own_part[b, y * n_inner + z] += up_in[b, z].astype(jnp.float32)

        @pl.when(z < n_inner - 1)
        def _():
            reduce_dn(b, z).wait_recv()
            own_part[b, y * n_inner + z] += dn_in[b, z].astype(jnp.float32)

        done = own_part[b, y * n_inner + z]
        last[0, b] = done[:tok]
        last[1, b] = done[tok:]
    to_last = send(last.at[1 - c], last_in, last_sem.at[0], last_sem.at[1], sibling)
    to_last.start()
    to_last.wait()
    for b in range(blocks):
        own, other = last[c, b], last_in[b]
        mixed_ref[:, b * wide : (b + 1) * wide] = jnp.where(c == 0, own, other).astype(jnp.bfloat16)
        mixed_ref[:, half + b * wide : half + (b + 1) * wide] = jnp.where(
            c == 0, other, own
        ).astype(jnp.bfloat16)

    for src in range(n_inner):

        @pl.when((z < n_inner - 1) & (src <= z))
        def _():
            gather_up(src).wait_send()

        @pl.when((z > 0) & (src >= z))
        def _():
            gather_dn(src).wait_send()

        gather_y(src).wait_send()
    for chunk in range(chunks):
        gather_sib(chunk).wait_send()
    for step in range(1, devices):
        sk_gather(step).wait_send()
    for b in range(blocks):
        to_sib(b).wait_send()
        for dest in range(n_inner):
            reduce_y(b, dest).wait_send()

            @pl.when(z < dest)
            def _():
                reduce_up(b, dest).wait_send()

            @pl.when(z > dest)
            def _():
                reduce_dn(b, dest).wait_send()


def gather_plan(
    quant_rows, block_scales, expert_ids, gate_scores, w_gate, w_up, w_down, sketch, owner_map
):
    n_expert = lax.axis_size("expert")
    n_inner = lax.axis_size("inner")
    devices = n_expert * n_inner
    chunks = devices // 2
    tok, width = quant_rows.shape
    experts = owner_map.shape[0]
    half = width // 2
    rows2 = 2 * tok
    total = devices * tok
    units = w_gate.shape[2]
    share, cols = sketch.shape[1:]
    group = total // n_inner
    blocks = BLOCKS
    wide = half // blocks
    bf16, f32 = jnp.bfloat16, jnp.float32
    vmem = pl.BlockSpec(memory_space=pltpu.VMEM)
    hbm = pl.BlockSpec(memory_space=pl.ANY)
    dma = pltpu.SemaphoreType.DMA
    flops = 2 * total * (3 * width * units + share * cols) + 2 * experts * total * cols * cols
    return pl.pallas_call(
        functools.partial(layer_kernel, n_inner, experts),
        out_shape=(
            jax.ShapeDtypeStruct((tok, width), bf16),
            jax.ShapeDtypeStruct((1, cols, cols), f32),
        ),
        in_specs=[vmem] * 4 + [hbm] * 4 + [pl.BlockSpec(memory_space=pltpu.SMEM)],
        out_specs=(vmem, vmem),
        scratch_shapes=[
            pltpu.VMEM((width, units), bf16),
            pltpu.VMEM((width, units), bf16),
            pltpu.VMEM((units, width), bf16),
            pltpu.VMEM((share, cols), bf16),
            pltpu.VMEM((2, tok, half + LANES), f32),
            pltpu.VMEM((tok, half + LANES), f32),
            pltpu.VMEM((2, chunks, rows2, half + LANES), bf16),
            pltpu.VMEM((n_inner, group, cols), bf16),
            pltpu.VMEM((n_inner, group, cols), bf16),
            pltpu.VMEM((devices, group, cols), bf16),
            pltpu.VMEM((total, units), bf16),
            pltpu.VMEM((blocks, chunks, rows2, wide), f32),
            pltpu.VMEM((blocks, chunks, rows2, wide), bf16),
            pltpu.VMEM((blocks, chunks, rows2, wide), bf16),
        ]
        + [pltpu.VMEM((blocks, n_inner, rows2, wide), bf16)] * 6
        + [
            pltpu.VMEM((2, blocks, tok, wide), f32),
            pltpu.VMEM((blocks, tok, wide), f32),
            dma((4,)),
            dma((2,)),
        ]
        + [dma((n_inner,))] * 6
        + [dma((chunks,))] * 2
        + [dma((n_inner,))] * 2
        + [dma((devices,))] * 2
        + [dma((blocks,))] * 2
        + [dma((blocks, n_inner))] * 6
        + [dma((2,))],
        cost_estimate=pl.CostEstimate(
            flops=flops,
            bytes_accessed=2 * (3 * width * units + share * cols),
            transcendentals=total * units,
        ),
        compiler_params=pltpu.CompilerParams(
            collective_id=0, has_side_effects=True, vmem_limit_bytes=56 * 1024 * 1024
        ),
    )(quant_rows, block_scales, expert_ids, gate_scores, w_gate, w_up, w_down, sketch, owner_map)


def per_device(
    quant_rows, block_scales, expert_ids, gate_scores, w_gate, w_up, w_down, sketch, owner_map
):
    plan = gather_plan if lax.axis_size("expert") == 4 else exchange_plan
    return plan(
        quant_rows, block_scales, expert_ids, gate_scores, w_gate, w_up, w_down, sketch, owner_map
    )


def solution(mesh):
    placed = (
        P(("groups", "expert", "inner"), None),
        P(("groups", "expert", "inner"), None),
        P(("groups", "expert", "inner"), None),
        P(("groups", "expert", "inner"), None),
        P("expert", None, "inner"),
        P("expert", None, "inner"),
        P("expert", "inner", None),
        P("expert", "inner", None),
        P(),
    )
    return jax.shard_map(
        per_device,
        mesh=mesh,
        in_specs=placed,
        out_specs=(
            P(("groups", "expert", "inner"), None),
            P(("groups", "expert", "inner"), None, None),
        ),
        check_vma=False,
    )
```

```python
import functools

import jax
import jax.numpy as jnp
from jax import lax
from jax.experimental import pallas as pl
from jax.experimental.pallas import tpu as pltpu
from jax.sharding import PartitionSpec as P

CAP = 5
BLOCKS = 2
LANES = 128
MESH = pl.DeviceIdType.MESH


def exchange_plan(
    quant_rows, block_scales, expert_ids, gate_scores, w_gate, w_up, w_down, sketch, owner_map
):
    n_expert = lax.axis_size("expert")
    n_inner = lax.axis_size("inner")
    all_blocks = n_expert * n_inner
    tok_count, top_count = expert_ids.shape
    model_width = quant_rows.shape[1]
    scale_cols = block_scales.shape[1]
    experts = owner_map.shape[0]
    sketch_cols = sketch.shape[2]
    total_rows = all_blocks * CAP
    flat_ids = expert_ids.reshape(-1)
    onehot = (flat_ids[:, None] == jnp.arange(experts, dtype=jnp.int32)[None, :]).astype(jnp.int32)
    slot_rank = jnp.sum((jnp.cumsum(onehot, axis=0) - onehot) * onehot, axis=1)
    source_token = jnp.arange(tok_count * top_count, dtype=jnp.int32) // top_count
    slot_table = (
        jnp.full((experts * CAP,), tok_count, jnp.int32)
        .at[flat_ids * CAP + slot_rank]
        .set(source_token)
    )
    padded_rows = jnp.concatenate([quant_rows, jnp.zeros((1, model_width), jnp.bfloat16)], axis=0)
    padded_scales = jnp.concatenate(
        [block_scales, jnp.zeros((1, scale_cols), jnp.bfloat16)], axis=0
    )
    send_rows = padded_rows[slot_table].reshape(experts, CAP, model_width)
    send_scales = padded_scales[slot_table].reshape(experts, CAP, scale_cols)
    wide_rows = jnp.broadcast_to(send_rows[:, None], (experts, n_inner, CAP, model_width))
    wide_scales = jnp.broadcast_to(send_scales[:, None], (experts, n_inner, CAP, scale_cols))
    inner_rows, inner_scales = (
        lax.all_to_all(
            wide_rows.reshape(all_blocks, CAP, model_width),
            ("expert", "inner"),
            split_axis=0,
            concat_axis=0,
            tiled=True,
        ),
        lax.all_to_all(
            wide_scales.reshape(all_blocks, CAP, scale_cols),
            ("expert", "inner"),
            split_axis=0,
            concat_axis=0,
            tiled=True,
        ),
    )
    expanded = inner_rows.reshape(total_rows, scale_cols, model_width // scale_cols).astype(
        jnp.float32
    )
    expanded = expanded * inner_scales.reshape(total_rows, scale_cols, 1).astype(jnp.float32)
    dequant = expanded.reshape(total_rows, model_width).astype(jnp.bfloat16)
    gate_w = w_gate[0]
    up_w = w_up[0]
    down_w = w_down[0]
    gate_proj = jnp.dot(dequant, gate_w, preferred_element_type=jnp.float32)
    up_proj = jnp.dot(dequant, up_w, preferred_element_type=jnp.float32)
    hidden = (jax.nn.silu(gate_proj) * up_proj).astype(jnp.bfloat16)
    partial_value = (
        jnp.dot(hidden, down_w, preferred_element_type=jnp.float32)
        .astype(jnp.bfloat16)
        .reshape(all_blocks, CAP, model_width)
    )
    returned = lax.all_to_all(
        partial_value, ("expert", "inner"), split_axis=0, concat_axis=0, tiled=True
    )
    returned = returned.reshape(n_expert, n_inner, CAP, model_width).astype(jnp.float32)
    outputs = jnp.sum(returned, axis=1).astype(jnp.bfloat16)
    picked = (
        outputs[flat_ids, slot_rank].reshape(tok_count, top_count, model_width).astype(jnp.float32)
    )
    totals = jnp.sum(gate_scores, axis=1, keepdims=True)
    weights = 2.5 * gate_scores / totals
    mixed = jnp.sum(picked * weights[:, :, None], axis=1).astype(jnp.bfloat16)
    part_rows = sketch.shape[1]
    first_col = lax.axis_index("inner") * part_rows
    column_part = lax.dynamic_slice_in_dim(dequant, first_col, part_rows, 1)
    sketched = lax.psum(
        jnp.dot(column_part, sketch[0], preferred_element_type=jnp.float32).astype(jnp.bfloat16),
        "inner",
    ).astype(jnp.float32)
    gram_local = jnp.dot(sketched.T, sketched, precision=lax.Precision.HIGHEST) / (
        tok_count * all_blocks
    )
    gram_all = lax.all_gather(
        gram_local[None].astype(jnp.bfloat16), "expert", axis=0, tiled=True
    ).astype(jnp.float32)
    own_rank = lax.axis_index("expert") * n_inner + lax.axis_index("inner")
    chosen = (owner_map == own_rank).astype(jnp.float32)
    gram_out = jnp.dot(
        chosen[None, :],
        gram_all.reshape(experts, sketch_cols * sketch_cols),
        precision=lax.Precision.HIGHEST,
    ).reshape(1, sketch_cols, sketch_cols)
    return (mixed, gram_out)


def layer_kernel(
    n_inner,
    experts,
    quant_ref,
    scale_ref,
    ids_ref,
    score_ref,
    gate_hbm,
    up_hbm,
    down_hbm,
    sketch_hbm,
    owner_ref,
    mixed_ref,
    gram_ref,
    gate_w,
    up_w,
    down_w,
    sketch_w,
    swap_out,
    swap_in,
    rows_first,
    rows_second,
    gate_sum,
    up_sum,
    sk_part,
    sk_in,
    sk_all,
    hidden,
    own_part,
    sib_out,
    sib_in,
    y_out,
    y_in,
    z_out,
    z_in,
    last,
    last_in,
    load_sem,
    swap_sem,
    zup_s,
    zup_r,
    zdn_s,
    zdn_r,
    yg_s,
    yg_r,
    sg_s,
    sg_r,
    skx_s,
    skx_r,
    ska_s,
    ska_r,
    sky,
    sib_s,
    sib_r,
    yr_s,
    yr_r,
    zr_s,
    zr_r,
    last_sem,
):
    expert = lax.axis_index("expert")
    z = lax.axis_index("inner")
    y, c = expert // 2, expert % 2
    sibling = {"expert": y * 2 + (1 - c), "inner": z}
    y_peer = {"expert": (1 - y) * 2 + c, "inner": z}
    above = {"expert": expert, "inner": lax.rem(z + 1, n_inner)}
    below = {"expert": expert, "inner": lax.rem(z + n_inner - 1, n_inner)}
    n_expert = 4
    devices = n_expert * n_inner
    chunks = 2 * n_inner
    tok = quant_ref.shape[0]
    width = quant_ref.shape[1]
    half = width // 2
    piece = half // 2
    rows = (rows_first, rows_second)
    blk = width // scale_ref.shape[1]
    total = chunks * 2 * tok
    rank = expert * n_inner + z

    def send(src, dst, send_sem, recv_sem, device):
        return pltpu.make_async_remote_copy(
            src_ref=src,
            dst_ref=dst,
            send_sem=send_sem,
            recv_sem=recv_sem,
            device_id=device,
            device_id_type=MESH,
        )

    loads = [
        pltpu.make_async_copy(sketch_hbm.at[0], sketch_w, load_sem.at[0]),
        pltpu.make_async_copy(gate_hbm.at[0], gate_w, load_sem.at[1]),
        pltpu.make_async_copy(up_hbm.at[0], up_w, load_sem.at[2]),
        pltpu.make_async_copy(down_hbm.at[0], down_w, load_sem.at[3]),
    ]

    barrier = pltpu.get_barrier_semaphore()
    for neighbour in (sibling, y_peer, above, below):
        pl.semaphore_signal(barrier, inc=1, device_id=neighbour, device_id_type=MESH)
    for load in loads:
        load.start()

    quant = quant_ref[...].astype(jnp.float32)
    scales = scale_ref[...].astype(jnp.float32)
    for j in range(width // blk):
        part = quant[:, j * blk : (j + 1) * blk] * scales[:, j : j + 1]
        h, col = divmod(j * blk, half)
        swap_out[h, :, col : col + blk] = part.astype(jnp.bfloat16).astype(jnp.float32)
    ids = ids_ref[...].astype(jnp.float32)
    scores = score_ref[...]
    weights = 2.5 * scores / jnp.sum(scores, axis=0, keepdims=True)
    diagonal = lax.broadcasted_iota(jnp.int32, (tok, tok), 0) == lax.broadcasted_iota(
        jnp.int32, (tok, tok), 1
    )

    def upright(row):
        spread = jnp.where(diagonal, jnp.broadcast_to(row, (tok, tok)), 0.0)
        return jnp.sum(spread, axis=1, keepdims=True)

    lane = lax.broadcasted_iota(jnp.int32, (tok, LANES), 1).astype(jnp.float32)
    meta = jnp.zeros((tok, LANES), jnp.float32)
    for k in range(ids.shape[0]):
        named = upright(ids[k : k + 1])
        value = upright(weights[k : k + 1])
        high = value.astype(jnp.bfloat16).astype(jnp.float32)
        meta = jnp.where(lane == named, high, meta)
        meta = jnp.where(lane == named + experts, value - high, meta)
        meta = jnp.where(lane == named + 2 * experts, 1.0, meta)
    for h in range(2):
        swap_out[h, :, half:] = meta

    pl.semaphore_wait(barrier, 4)

    swap = send(swap_out.at[1 - c], swap_in, swap_sem.at[0], swap_sem.at[1], sibling)
    swap.start()
    swap.wait()
    mine = y * n_inner + z

    def place(h, low, high):
        pair = jnp.concatenate([low, high], axis=0).astype(jnp.bfloat16)
        rows[0][h, mine, :, :piece] = pair[:, :piece]
        rows[0][h, mine, :, piece:] = pair[:, half:]
        rows[1][h, mine] = pair[:, piece:half]

    @pl.when(c == 0)
    def _():
        place(0, swap_out[0], swap_in[...])

    @pl.when(c == 1)
    def _():
        place(1, swap_in[...], swap_out[1])

    def gather_up(p, src):
        ref = rows[p].at[c, y * n_inner + src]
        return send(ref, ref, zup_s.at[p, src], zup_r.at[p, src], above)

    def gather_dn(p, src):
        ref = rows[p].at[c, y * n_inner + src]
        return send(ref, ref, zdn_s.at[p, src], zdn_r.at[p, src], below)

    def gather_y(p, src):
        ref = rows[p].at[c, y * n_inner + src]
        return send(ref, ref, yg_s.at[p, src], yg_r.at[p, src], y_peer)

    def from_y(p, src):
        ref = rows[p].at[c, (1 - y) * n_inner + src]
        return send(ref, ref, yg_s.at[p, src], yg_r.at[p, src], y_peer)

    def gather_sib(p, chunk):
        ref = rows[p].at[c, chunk]
        return send(ref, ref, sg_s.at[p, chunk], sg_r.at[p, chunk], sibling)

    def from_sib(p, chunk):
        ref = rows[p].at[1 - c, chunk]
        return send(ref, ref, sg_s.at[p, chunk], sg_r.at[p, chunk], sibling)

    def own(p):
        @pl.when(z < n_inner - 1)
        def _():
            gather_up(p, z).start()

        @pl.when(z > 0)
        def _():
            gather_dn(p, z).start()

        gather_y(p, z).start()
        gather_sib(p, mine).start()

    def z_step(p, s):
        @pl.when(z - s >= 0)
        def _():
            src = lax.rem(z - s + n_inner, n_inner)
            gather_up(p, src).wait_recv()

            @pl.when(z < n_inner - 1)
            def _():
                gather_up(p, src).start()

            gather_y(p, src).start()
            gather_sib(p, y * n_inner + src).start()

        @pl.when(z + s < n_inner)
        def _():
            src = lax.rem(z + s, n_inner)
            gather_dn(p, src).wait_recv()

            @pl.when(z > 0)
            def _():
                gather_dn(p, src).start()

            gather_y(p, src).start()
            gather_sib(p, y * n_inner + src).start()

    def when_y(p, src):
        from_y(p, src).wait_recv()
        gather_sib(p, (1 - y) * n_inner + src).start()

    def y_step(p, s):
        if s == 0:
            when_y(p, z)
            return

        @pl.when(z - s >= 0)
        def _():
            when_y(p, lax.rem(z - s + n_inner, n_inner))

        @pl.when(z + s < n_inner)
        def _():
            when_y(p, lax.rem(z + s, n_inner))

    tile = 256
    tiles = hidden.shape[1] // tile

    def project(p, n):
        at = slice(n * tile, (n + 1) * tile)
        sums = []
        for w in (gate_w, up_w):
            part = 0.0
            for h in range(2):
                x = rows[p][h, :, :, :piece].reshape(total, piece)
                low = h * half + p * piece
                part += jnp.dot(x, w[low : low + piece, at], preferred_element_type=jnp.float32)
            sums.append(part)
        if p == 0:
            gate_sum[:, at], up_sum[:, at] = sums
        else:
            gate, up = gate_sum[:, at] + sums[0], up_sum[:, at] + sums[1]
            hidden[:, at] = (gate / (1.0 + jnp.exp(-gate)) * up).astype(jnp.bfloat16)

    own(0)
    own(1)
    for s in range(1, n_inner):
        for p in range(2):
            z_step(p, s)
    for s in range(n_inner - 1):
        for p in range(2):
            y_step(p, s)
    y_step(0, n_inner - 1)
    for chunk in range(chunks):
        from_sib(0, chunk).wait_recv()
    loads[1].wait()
    loads[2].wait()
    project(0, 0)
    y_step(1, n_inner - 1)
    for n in range(1, tiles):
        project(0, n)
    for chunk in range(chunks):
        from_sib(1, chunk).wait_recv()

    info = rows[0][0, :, :, piece:].reshape(total, LANES).astype(jnp.float32)
    lanes = lax.broadcasted_iota(jnp.int32, (total, LANES), 1)

    def column(index):
        return jnp.sum(jnp.where(lanes == index, info, 0.0), axis=1, keepdims=True)

    weight = column(expert) + column(expert + experts)
    routed = column(expert + 2 * experts)

    loads[0].wait()
    h = z // 2
    columns = jnp.where(lax.rem(z, 2) == 0, rows[0][h, :, :, :piece], rows[1][h])
    columns = columns.reshape(total, piece)
    product = jnp.dot(columns, sketch_w[...], preferred_element_type=jnp.float32) * routed
    cols = product.shape[1]
    group = total // n_inner
    sk_part[...] = product.astype(jnp.bfloat16).reshape(n_inner, group, cols)

    def sk_exchange(step):
        to = lax.rem(z + step, n_inner)
        return send(
            sk_part.at[to],
            sk_in.at[step],
            skx_s.at[step],
            skx_r.at[step],
            {"expert": expert, "inner": to},
        )

    for step in range(1, n_inner):
        sk_exchange(step).start()

    project(1, 0)

    summed = sk_part[z].astype(jnp.float32)
    for step in range(1, n_inner):
        sk_exchange(step).wait()
        summed += sk_in[step].astype(jnp.float32)
    sk_all[rank] = summed.astype(jnp.bfloat16)

    def sk_along(step):
        return send(
            sk_all.at[rank],
            sk_all.at[rank],
            ska_s.at[step],
            ska_r.at[step],
            {"expert": expert, "inner": lax.rem(z + step, n_inner)},
        )

    def sk_landed(step):
        ref = sk_all.at[expert * n_inner + lax.rem(z - step + n_inner, n_inner)]
        return send(ref, ref, ska_s.at[step], ska_r.at[step], sibling)

    def sk_block(of):
        return sk_all.at[pl.ds(of * n_inner, n_inner)]

    far = (1 - y) * 2 + c
    twin = y * 2 + 1 - c
    sk_to_y = send(sk_block(expert), sk_block(expert), sky.at[0], sky.at[1], y_peer)
    sk_from_y = send(sk_block(far), sk_block(far), sky.at[0], sky.at[1], y_peer)
    sk_near = send(sk_block(expert), sk_block(expert), sky.at[2], sky.at[3], sibling)
    sk_from_near = send(sk_block(twin), sk_block(twin), sky.at[2], sky.at[3], sibling)
    sk_far = send(sk_block(far), sk_block(far), sky.at[4], sky.at[5], sibling)
    cross = (1 - y) * 2 + 1 - c
    sk_from_far = send(sk_block(cross), sk_block(cross), sky.at[4], sky.at[5], sibling)

    for step in range(1, n_inner):
        sk_along(step).start()

    for n in range(1, tiles):
        project(1, n)

    for step in range(1, n_inner):
        sk_landed(step).wait_recv()
    sk_to_y.start()
    sk_near.start()

    loads[3].wait()
    blocks, _, _, wide = own_part.shape

    def down(h, b):
        at = pl.ds(pl.multiple_of(h * half + b * wide, LANES), wide)
        out = jnp.dot(hidden[...], down_w[:, at], preferred_element_type=jnp.float32)
        return (out * weight).reshape(chunks, 2 * tok, wide)

    def to_sib(b):
        return send(sib_out.at[b], sib_in.at[b], sib_s.at[b], sib_r.at[b], sibling)

    def reduce_y(b, dest):
        return send(y_out.at[b, dest], y_in.at[b, dest], yr_s.at[b, dest], yr_r.at[b, dest], y_peer)

    def reduce_z(b, step):
        return send(
            z_out.at[b, step],
            z_in.at[b, step],
            zr_s.at[b, step],
            zr_r.at[b, step],
            {"expert": expert, "inner": lax.rem(z + step, n_inner)},
        )

    def chip_sum(b, y_to, dest):
        at = y_to * n_inner + dest
        return own_part[b, at] + sib_in[b, at].astype(jnp.float32)

    order = [n_inner // 2] + [s for s in range(1, n_inner) if s != n_inner // 2] + [0]

    def start_y(b):
        to_sib(b).wait_recv()
        for step in order:
            dest = lax.rem(z + step, n_inner)
            y_out[b, dest] = chip_sum(b, 1 - y, dest).astype(jnp.bfloat16)
            reduce_y(b, dest).start()

    for b in range(blocks):
        sib_out[b] = down(1 - c, b).astype(jnp.bfloat16)
        to_sib(b).start()
        own_part[b] = down(c, b)
        start_y(b)

    def plane_sum(b, dest):
        reduce_y(b, dest).wait_recv()
        return chip_sum(b, y, dest) + y_in[b, dest].astype(jnp.float32)

    for b in range(blocks):
        for step in order[:-1]:
            dest = lax.rem(z + step, n_inner)
            z_out[b, step] = plane_sum(b, dest).astype(jnp.bfloat16)
            reduce_z(b, step).start()
        if b == 0:
            sk_from_y.wait_recv()
            sk_far.start()

    sk_from_near.wait_recv()
    sk_from_far.wait_recv()
    gram = jnp.zeros((cols, cols), jnp.float32)
    for e in range(experts):
        chosen = jnp.where(owner_ref[e] == rank, 1.0 / total, 0.0).astype(jnp.float32)
        part = sk_all[e * n_inner : (e + 1) * n_inner].reshape(total, cols)
        gram += chosen * lax.dot_general(
            part, part, (((0,), (0,)), ((), ())), preferred_element_type=jnp.float32
        )
    gram_ref[0] = gram

    for b in range(blocks):
        done = plane_sum(b, z)
        for step in order[:-1]:
            reduce_z(b, step).wait_recv()
            done += z_in[b, step].astype(jnp.float32)
        last[0, b] = done[:tok]
        last[1, b] = done[tok:]
    to_last = send(last.at[1 - c], last_in, last_sem.at[0], last_sem.at[1], sibling)
    to_last.start()
    to_last.wait()
    for b in range(blocks):
        own, other = last[c, b], last_in[b]
        mixed_ref[:, b * wide : (b + 1) * wide] = jnp.where(c == 0, own, other).astype(jnp.bfloat16)
        mixed_ref[:, half + b * wide : half + (b + 1) * wide] = jnp.where(
            c == 0, other, own
        ).astype(jnp.bfloat16)

    for p in range(2):
        for src in range(n_inner):

            @pl.when((z < n_inner - 1) & (src <= z))
            def _():
                gather_up(p, src).wait_send()

            @pl.when((z > 0) & (src >= z))
            def _():
                gather_dn(p, src).wait_send()

            gather_y(p, src).wait_send()
        for chunk in range(chunks):
            gather_sib(p, chunk).wait_send()
    for step in range(1, n_inner):
        sk_along(step).wait_send()
    sk_to_y.wait_send()
    sk_near.wait_send()
    sk_far.wait_send()
    for b in range(blocks):
        to_sib(b).wait_send()
        for dest in range(n_inner):
            reduce_y(b, dest).wait_send()
        for step in range(1, n_inner):
            reduce_z(b, step).wait_send()


def gather_plan(
    quant_rows, block_scales, expert_ids, gate_scores, w_gate, w_up, w_down, sketch, owner_map
):
    n_expert = lax.axis_size("expert")
    n_inner = lax.axis_size("inner")
    devices = n_expert * n_inner
    chunks = devices // 2
    tok, width = quant_rows.shape
    experts = owner_map.shape[0]
    half = width // 2
    rows2 = 2 * tok
    total = devices * tok
    units = w_gate.shape[2]
    share, cols = sketch.shape[1:]
    group = total // n_inner
    blocks = BLOCKS
    wide = half // blocks
    bf16, f32 = jnp.bfloat16, jnp.float32
    vmem = pl.BlockSpec(memory_space=pltpu.VMEM)
    hbm = pl.BlockSpec(memory_space=pl.ANY)
    dma = pltpu.SemaphoreType.DMA
    flops = 2 * total * (3 * width * units + share * cols) + 2 * experts * total * cols * cols
    return pl.pallas_call(
        functools.partial(layer_kernel, n_inner, experts),
        out_shape=(
            jax.ShapeDtypeStruct((tok, width), bf16),
            jax.ShapeDtypeStruct((1, cols, cols), f32),
        ),
        in_specs=[vmem] * 4 + [hbm] * 4 + [pl.BlockSpec(memory_space=pltpu.SMEM)],
        out_specs=(vmem, vmem),
        scratch_shapes=[
            pltpu.VMEM((width, units), bf16),
            pltpu.VMEM((width, units), bf16),
            pltpu.VMEM((units, width), bf16),
            pltpu.VMEM((share, cols), bf16),
            pltpu.VMEM((2, tok, half + LANES), f32),
            pltpu.VMEM((tok, half + LANES), f32),
            pltpu.VMEM((2, chunks, rows2, half // 2 + LANES), bf16),
            pltpu.VMEM((2, chunks, rows2, half // 2), bf16),
            pltpu.VMEM((total, units), f32),
            pltpu.VMEM((total, units), f32),
            pltpu.VMEM((n_inner, group, cols), bf16),
            pltpu.VMEM((n_inner, group, cols), bf16),
            pltpu.VMEM((devices, group, cols), bf16),
            pltpu.VMEM((total, units), bf16),
            pltpu.VMEM((blocks, chunks, rows2, wide), f32),
            pltpu.VMEM((blocks, chunks, rows2, wide), bf16),
            pltpu.VMEM((blocks, chunks, rows2, wide), bf16),
        ]
        + [pltpu.VMEM((blocks, n_inner, rows2, wide), bf16)] * 4
        + [
            pltpu.VMEM((2, blocks, tok, wide), f32),
            pltpu.VMEM((blocks, tok, wide), f32),
            dma((4,)),
            dma((2,)),
        ]
        + [dma((2, n_inner))] * 6
        + [dma((2, chunks))] * 2
        + [dma((n_inner,))] * 4
        + [dma((6,))]
        + [dma((blocks,))] * 2
        + [dma((blocks, n_inner))] * 4
        + [dma((2,))],
        cost_estimate=pl.CostEstimate(
            flops=flops,
            bytes_accessed=2 * (3 * width * units + share * cols),
            transcendentals=total * units,
        ),
        compiler_params=pltpu.CompilerParams(
            collective_id=0, has_side_effects=True, vmem_limit_bytes=56 * 1024 * 1024
        ),
    )(quant_rows, block_scales, expert_ids.T, gate_scores.T, w_gate, w_up, w_down, sketch, owner_map)


def per_device(
    quant_rows, block_scales, expert_ids, gate_scores, w_gate, w_up, w_down, sketch, owner_map
):
    small = lax.axis_size("expert") == 4 and lax.axis_size("inner") == 4
    plan = gather_plan if small else exchange_plan
    return plan(
        quant_rows, block_scales, expert_ids, gate_scores, w_gate, w_up, w_down, sketch, owner_map
    )


def solution(mesh):
    placed = (
        P(("groups", "expert", "inner"), None),
        P(("groups", "expert", "inner"), None),
        P(("groups", "expert", "inner"), None),
        P(("groups", "expert", "inner"), None),
        P("expert", None, "inner"),
        P("expert", None, "inner"),
        P("expert", "inner", None),
        P("expert", "inner", None),
        P(),
    )
    return jax.shard_map(
        per_device,
        mesh=mesh,
        in_specs=placed,
        out_specs=(
            P(("groups", "expert", "inner"), None),
            P(("groups", "expert", "inner"), None, None),
        ),
        check_vma=False,
    )
```

```python
import functools

import jax
import jax.numpy as jnp
from jax import lax
from jax.experimental import pallas as pl
from jax.experimental.pallas import tpu as pltpu
from jax.sharding import PartitionSpec as P

CAP = 5
BLOCKS = 2
LANES = 128
MESH = pl.DeviceIdType.MESH


def exchange_plan(
    quant_rows, block_scales, expert_ids, gate_scores, w_gate, w_up, w_down, sketch, owner_map
):
    n_expert = lax.axis_size("expert")
    n_inner = lax.axis_size("inner")
    all_blocks = n_expert * n_inner
    tok_count, top_count = expert_ids.shape
    model_width = quant_rows.shape[1]
    scale_cols = block_scales.shape[1]
    experts = owner_map.shape[0]
    sketch_cols = sketch.shape[2]
    total_rows = all_blocks * CAP
    flat_ids = expert_ids.reshape(-1)
    onehot = (flat_ids[:, None] == jnp.arange(experts, dtype=jnp.int32)[None, :]).astype(jnp.int32)
    slot_rank = jnp.sum((jnp.cumsum(onehot, axis=0) - onehot) * onehot, axis=1)
    source_token = jnp.arange(tok_count * top_count, dtype=jnp.int32) // top_count
    slot_table = (
        jnp.full((experts * CAP,), tok_count, jnp.int32)
        .at[flat_ids * CAP + slot_rank]
        .set(source_token)
    )
    padded_rows = jnp.concatenate([quant_rows, jnp.zeros((1, model_width), jnp.bfloat16)], axis=0)
    padded_scales = jnp.concatenate(
        [block_scales, jnp.zeros((1, scale_cols), jnp.bfloat16)], axis=0
    )
    send_rows = padded_rows[slot_table].reshape(experts, CAP, model_width)
    send_scales = padded_scales[slot_table].reshape(experts, CAP, scale_cols)
    wide_rows = jnp.broadcast_to(send_rows[:, None], (experts, n_inner, CAP, model_width))
    wide_scales = jnp.broadcast_to(send_scales[:, None], (experts, n_inner, CAP, scale_cols))
    inner_rows, inner_scales = (
        lax.all_to_all(
            wide_rows.reshape(all_blocks, CAP, model_width),
            ("expert", "inner"),
            split_axis=0,
            concat_axis=0,
            tiled=True,
        ),
        lax.all_to_all(
            wide_scales.reshape(all_blocks, CAP, scale_cols),
            ("expert", "inner"),
            split_axis=0,
            concat_axis=0,
            tiled=True,
        ),
    )
    expanded = inner_rows.reshape(total_rows, scale_cols, model_width // scale_cols).astype(
        jnp.float32
    )
    expanded = expanded * inner_scales.reshape(total_rows, scale_cols, 1).astype(jnp.float32)
    dequant = expanded.reshape(total_rows, model_width).astype(jnp.bfloat16)
    gate_w = w_gate[0]
    up_w = w_up[0]
    down_w = w_down[0]
    gate_proj = jnp.dot(dequant, gate_w, preferred_element_type=jnp.float32)
    up_proj = jnp.dot(dequant, up_w, preferred_element_type=jnp.float32)
    hidden = (jax.nn.silu(gate_proj) * up_proj).astype(jnp.bfloat16)
    partial_value = (
        jnp.dot(hidden, down_w, preferred_element_type=jnp.float32)
        .astype(jnp.bfloat16)
        .reshape(all_blocks, CAP, model_width)
    )
    returned = lax.all_to_all(
        partial_value, ("expert", "inner"), split_axis=0, concat_axis=0, tiled=True
    )
    returned = returned.reshape(n_expert, n_inner, CAP, model_width).astype(jnp.float32)
    outputs = jnp.sum(returned, axis=1).astype(jnp.bfloat16)
    picked = (
        outputs[flat_ids, slot_rank].reshape(tok_count, top_count, model_width).astype(jnp.float32)
    )
    totals = jnp.sum(gate_scores, axis=1, keepdims=True)
    weights = 2.5 * gate_scores / totals
    mixed = jnp.sum(picked * weights[:, :, None], axis=1).astype(jnp.bfloat16)
    part_rows = sketch.shape[1]
    first_col = lax.axis_index("inner") * part_rows
    column_part = lax.dynamic_slice_in_dim(dequant, first_col, part_rows, 1)
    sketched = lax.psum(
        jnp.dot(column_part, sketch[0], preferred_element_type=jnp.float32).astype(jnp.bfloat16),
        "inner",
    ).astype(jnp.float32)
    gram_local = jnp.dot(sketched.T, sketched, precision=lax.Precision.HIGHEST) / (
        tok_count * all_blocks
    )
    gram_all = lax.all_gather(
        gram_local[None].astype(jnp.bfloat16), "expert", axis=0, tiled=True
    ).astype(jnp.float32)
    own_rank = lax.axis_index("expert") * n_inner + lax.axis_index("inner")
    chosen = (owner_map == own_rank).astype(jnp.float32)
    gram_out = jnp.dot(
        chosen[None, :],
        gram_all.reshape(experts, sketch_cols * sketch_cols),
        precision=lax.Precision.HIGHEST,
    ).reshape(1, sketch_cols, sketch_cols)
    return (mixed, gram_out)


def layer_kernel(
    n_inner,
    experts,
    quant_ref,
    scale_ref,
    ids_ref,
    score_ref,
    gate_hbm,
    up_hbm,
    down_hbm,
    sketch_hbm,
    owner_ref,
    mixed_ref,
    gram_ref,
    gate_w,
    up_w,
    down_w,
    sketch_w,
    swap_out,
    swap_in,
    rows_first,
    rows_second,
    gate_sum,
    up_sum,
    sk_part,
    sk_in,
    sk_all,
    hidden,
    own_part,
    sib_out,
    sib_in,
    y_out,
    y_in,
    z_out,
    z_in,
    last,
    last_in,
    load_sem,
    swap_sem,
    zup_s,
    zup_r,
    zdn_s,
    zdn_r,
    yg_s,
    yg_r,
    sg_s,
    sg_r,
    skx_s,
    skx_r,
    ska_s,
    ska_r,
    sky,
    sib_s,
    sib_r,
    yr_s,
    yr_r,
    zr_s,
    zr_r,
    last_sem,
):
    expert = lax.axis_index("expert")
    z = lax.axis_index("inner")
    y, c = expert // 2, expert % 2
    sibling = {"expert": y * 2 + (1 - c), "inner": z}
    y_peer = {"expert": (1 - y) * 2 + c, "inner": z}
    above = {"expert": expert, "inner": lax.rem(z + 1, n_inner)}
    below = {"expert": expert, "inner": lax.rem(z + n_inner - 1, n_inner)}
    n_expert = 4
    devices = n_expert * n_inner
    chunks = 2 * n_inner
    tok = quant_ref.shape[0]
    width = quant_ref.shape[1]
    half = width // 2
    piece = half // 2
    rows = (rows_first, rows_second)
    blk = width // scale_ref.shape[1]
    total = chunks * 2 * tok
    rank = expert * n_inner + z

    def send(src, dst, send_sem, recv_sem, device):
        return pltpu.make_async_remote_copy(
            src_ref=src,
            dst_ref=dst,
            send_sem=send_sem,
            recv_sem=recv_sem,
            device_id=device,
            device_id_type=MESH,
        )

    loads = [
        pltpu.make_async_copy(sketch_hbm.at[0], sketch_w, load_sem.at[0]),
        pltpu.make_async_copy(gate_hbm.at[0], gate_w, load_sem.at[1]),
        pltpu.make_async_copy(up_hbm.at[0], up_w, load_sem.at[2]),
        pltpu.make_async_copy(down_hbm.at[0], down_w, load_sem.at[3]),
    ]

    barrier = pltpu.get_barrier_semaphore()
    for neighbour in (sibling, y_peer, above, below):
        pl.semaphore_signal(barrier, inc=1, device_id=neighbour, device_id_type=MESH)
    for load in loads:
        load.start()

    quant = quant_ref[...].astype(jnp.float32)
    scales = scale_ref[...].astype(jnp.float32)
    for j in range(width // blk):
        part = quant[:, j * blk : (j + 1) * blk] * scales[:, j : j + 1]
        h, col = divmod(j * blk, half)
        swap_out[h, :, col : col + blk] = part.astype(jnp.bfloat16).astype(jnp.float32)
    ids = ids_ref[...].astype(jnp.float32)
    scores = score_ref[...]
    weights = 2.5 * scores / jnp.sum(scores, axis=0, keepdims=True)
    diagonal = lax.broadcasted_iota(jnp.int32, (tok, tok), 0) == lax.broadcasted_iota(
        jnp.int32, (tok, tok), 1
    )

    def upright(row):
        spread = jnp.where(diagonal, jnp.broadcast_to(row, (tok, tok)), 0.0)
        return jnp.sum(spread, axis=1, keepdims=True)

    lane = lax.broadcasted_iota(jnp.int32, (tok, LANES), 1).astype(jnp.float32)
    meta = jnp.zeros((tok, LANES), jnp.float32)
    for k in range(ids.shape[0]):
        named = upright(ids[k : k + 1])
        value = upright(weights[k : k + 1])
        high = value.astype(jnp.bfloat16).astype(jnp.float32)
        meta = jnp.where(lane == named, high, meta)
        meta = jnp.where(lane == named + experts, value - high, meta)
        meta = jnp.where(lane == named + 2 * experts, 1.0, meta)
    for h in range(2):
        swap_out[h, :, half:] = meta

    pl.semaphore_wait(barrier, 4)

    swap = send(swap_out.at[1 - c], swap_in, swap_sem.at[0], swap_sem.at[1], sibling)
    swap.start()
    swap.wait()
    mine = y * n_inner + z

    def place(h, low, high):
        pair = jnp.concatenate([low, high], axis=0).astype(jnp.bfloat16)
        rows[0][h, mine, :, :piece] = pair[:, :piece]
        rows[0][h, mine, :, piece:] = pair[:, half:]
        rows[1][h, mine] = pair[:, piece:half]

    @pl.when(c == 0)
    def _():
        place(0, swap_out[0], swap_in[...])

    @pl.when(c == 1)
    def _():
        place(1, swap_in[...], swap_out[1])

    def gather_up(p, src):
        ref = rows[p].at[c, y * n_inner + src]
        return send(ref, ref, zup_s.at[p, src], zup_r.at[p, src], above)

    def gather_dn(p, src):
        ref = rows[p].at[c, y * n_inner + src]
        return send(ref, ref, zdn_s.at[p, src], zdn_r.at[p, src], below)

    def gather_y(p, src):
        ref = rows[p].at[c, y * n_inner + src]
        return send(ref, ref, yg_s.at[p, src], yg_r.at[p, src], y_peer)

    def from_y(p, src):
        ref = rows[p].at[c, (1 - y) * n_inner + src]
        return send(ref, ref, yg_s.at[p, src], yg_r.at[p, src], y_peer)

    def gather_sib(p, chunk):
        ref = rows[p].at[c, chunk]
        return send(ref, ref, sg_s.at[p, chunk], sg_r.at[p, chunk], sibling)

    def from_sib(p, chunk):
        ref = rows[p].at[1 - c, chunk]
        return send(ref, ref, sg_s.at[p, chunk], sg_r.at[p, chunk], sibling)

    def own(p):
        @pl.when(z < n_inner - 1)
        def _():
            gather_up(p, z).start()

        @pl.when(z > 0)
        def _():
            gather_dn(p, z).start()

        gather_y(p, z).start()
        gather_sib(p, mine).start()

    def z_step(p, s):
        @pl.when(z - s >= 0)
        def _():
            src = lax.rem(z - s + n_inner, n_inner)
            gather_up(p, src).wait_recv()

            @pl.when(z < n_inner - 1)
            def _():
                gather_up(p, src).start()

            gather_y(p, src).start()
            gather_sib(p, y * n_inner + src).start()

        @pl.when(z + s < n_inner)
        def _():
            src = lax.rem(z + s, n_inner)
            gather_dn(p, src).wait_recv()

            @pl.when(z > 0)
            def _():
                gather_dn(p, src).start()

            gather_y(p, src).start()
            gather_sib(p, y * n_inner + src).start()

    def when_y(p, src):
        from_y(p, src).wait_recv()
        gather_sib(p, (1 - y) * n_inner + src).start()

    def y_step(p, s):
        if s == 0:
            when_y(p, z)
            return

        @pl.when(z - s >= 0)
        def _():
            when_y(p, lax.rem(z - s + n_inner, n_inner))

        @pl.when(z + s < n_inner)
        def _():
            when_y(p, lax.rem(z + s, n_inner))

    tile = 256
    tiles = hidden.shape[1] // tile

    def project(p, n):
        at = slice(n * tile, (n + 1) * tile)
        sums = []
        for w in (gate_w, up_w):
            part = 0.0
            for h in range(2):
                x = rows[p][h, :, :, :piece].reshape(total, piece)
                low = h * half + p * piece
                part += jnp.dot(x, w[low : low + piece, at], preferred_element_type=jnp.float32)
            sums.append(part)
        if p == 0:
            gate_sum[:, at], up_sum[:, at] = sums
        else:
            gate, up = gate_sum[:, at] + sums[0], up_sum[:, at] + sums[1]
            hidden[:, at] = (gate / (1.0 + jnp.exp(-gate)) * up).astype(jnp.bfloat16)

    own(0)
    own(1)
    for s in range(1, n_inner):
        for p in range(2):
            z_step(p, s)
    for s in range(n_inner - 1):
        for p in range(2):
            y_step(p, s)
    y_step(0, n_inner - 1)
    for chunk in range(chunks):
        from_sib(0, chunk).wait_recv()
    loads[1].wait()
    loads[2].wait()
    project(0, 0)
    y_step(1, n_inner - 1)
    for n in range(1, tiles):
        project(0, n)
    for chunk in range(chunks):
        from_sib(1, chunk).wait_recv()

    info = rows[0][0, :, :, piece:].reshape(total, LANES).astype(jnp.float32)
    lanes = lax.broadcasted_iota(jnp.int32, (total, LANES), 1)

    def column(index):
        return jnp.sum(jnp.where(lanes == index, info, 0.0), axis=1, keepdims=True)

    weight = column(expert) + column(expert + experts)
    routed = column(expert + 2 * experts)

    loads[0].wait()
    h = z // 2
    columns = jnp.where(lax.rem(z, 2) == 0, rows[0][h, :, :, :piece], rows[1][h])
    columns = columns.reshape(total, piece)
    product = jnp.dot(columns, sketch_w[...], preferred_element_type=jnp.float32) * routed
    cols = product.shape[1]
    group = total // n_inner
    sk_part[...] = product.astype(jnp.bfloat16).reshape(n_inner, group, cols)

    def sk_exchange(step):
        to = lax.rem(z + step, n_inner)
        return send(
            sk_part.at[to],
            sk_in.at[step],
            skx_s.at[step],
            skx_r.at[step],
            {"expert": expert, "inner": to},
        )

    for step in range(1, n_inner):
        sk_exchange(step).start()

    for n in range(tiles):
        project(1, n)

    summed = sk_part[z].astype(jnp.float32)
    for step in range(1, n_inner):
        sk_exchange(step).wait()
        summed += sk_in[step].astype(jnp.float32)
    sk_all[rank] = summed.astype(jnp.bfloat16)

    def sk_along(step):
        return send(
            sk_all.at[rank],
            sk_all.at[rank],
            ska_s.at[step],
            ska_r.at[step],
            {"expert": expert, "inner": lax.rem(z + step, n_inner)},
        )

    def sk_landed(step):
        ref = sk_all.at[expert * n_inner + lax.rem(z - step + n_inner, n_inner)]
        return send(ref, ref, ska_s.at[step], ska_r.at[step], sibling)

    def sk_block(of):
        return sk_all.at[pl.ds(of * n_inner, n_inner)]

    far = (1 - y) * 2 + c
    twin = y * 2 + 1 - c
    sk_to_y = send(sk_block(expert), sk_block(expert), sky.at[0], sky.at[1], y_peer)
    sk_from_y = send(sk_block(far), sk_block(far), sky.at[0], sky.at[1], y_peer)
    sk_near = send(sk_block(expert), sk_block(expert), sky.at[2], sky.at[3], sibling)
    sk_from_near = send(sk_block(twin), sk_block(twin), sky.at[2], sky.at[3], sibling)
    sk_far = send(sk_block(far), sk_block(far), sky.at[4], sky.at[5], sibling)
    cross = (1 - y) * 2 + 1 - c
    sk_from_far = send(sk_block(cross), sk_block(cross), sky.at[4], sky.at[5], sibling)

    for step in range(1, n_inner):
        sk_along(step).start()

    loads[3].wait()
    blocks, _, _, wide = own_part.shape

    def down(h, b):
        at = pl.ds(pl.multiple_of(h * half + b * wide, LANES), wide)
        out = jnp.dot(hidden[...], down_w[:, at], preferred_element_type=jnp.float32)
        return (out * weight).reshape(chunks, 2 * tok, wide)

    def to_sib(b):
        return send(sib_out.at[b], sib_in.at[b], sib_s.at[b], sib_r.at[b], sibling)

    def reduce_y(b, dest):
        return send(y_out.at[b, dest], y_in.at[b, dest], yr_s.at[b, dest], yr_r.at[b, dest], y_peer)

    def reduce_z(b, step):
        return send(
            z_out.at[b, step],
            z_in.at[b, step],
            zr_s.at[b, step],
            zr_r.at[b, step],
            {"expert": expert, "inner": lax.rem(z + step, n_inner)},
        )

    def chip_sum(b, y_to, dest):
        at = y_to * n_inner + dest
        return own_part[b, at] + sib_in[b, at].astype(jnp.float32)

    order = [n_inner // 2] + [s for s in range(1, n_inner) if s != n_inner // 2] + [0]

    def start_y(b):
        to_sib(b).wait_recv()
        for step in order:
            dest = lax.rem(z + step, n_inner)
            y_out[b, dest] = chip_sum(b, 1 - y, dest).astype(jnp.bfloat16)
            reduce_y(b, dest).start()

    for b in range(blocks):
        sib_out[b] = down(1 - c, b).astype(jnp.bfloat16)
        to_sib(b).start()
        own_part[b] = down(c, b)
        start_y(b)
        if b == 0:
            for step in range(1, n_inner):
                sk_landed(step).wait_recv()
            sk_to_y.start()
            sk_near.start()

    def plane_sum(b, dest):
        reduce_y(b, dest).wait_recv()
        return chip_sum(b, y, dest) + y_in[b, dest].astype(jnp.float32)

    for b in range(blocks):
        for step in order[:-1]:
            dest = lax.rem(z + step, n_inner)
            z_out[b, step] = plane_sum(b, dest).astype(jnp.bfloat16)
            reduce_z(b, step).start()
        if b == 0:
            sk_from_y.wait_recv()
            sk_far.start()

    sk_from_near.wait_recv()
    sk_from_far.wait_recv()
    gram = jnp.zeros((cols, cols), jnp.float32)
    for e in range(experts):
        chosen = jnp.where(owner_ref[e] == rank, 1.0 / total, 0.0).astype(jnp.float32)
        part = sk_all[e * n_inner : (e + 1) * n_inner].reshape(total, cols)
        gram += chosen * lax.dot_general(
            part, part, (((0,), (0,)), ((), ())), preferred_element_type=jnp.float32
        )
    gram_ref[0] = gram

    for b in range(blocks):
        done = plane_sum(b, z)
        for step in order[:-1]:
            reduce_z(b, step).wait_recv()
            done += z_in[b, step].astype(jnp.float32)
        last[0, b] = done[:tok]
        last[1, b] = done[tok:]
    to_last = send(last.at[1 - c], last_in, last_sem.at[0], last_sem.at[1], sibling)
    to_last.start()
    to_last.wait()
    for b in range(blocks):
        own, other = last[c, b], last_in[b]
        mixed_ref[:, b * wide : (b + 1) * wide] = jnp.where(c == 0, own, other).astype(jnp.bfloat16)
        mixed_ref[:, half + b * wide : half + (b + 1) * wide] = jnp.where(
            c == 0, other, own
        ).astype(jnp.bfloat16)

    for p in range(2):
        for src in range(n_inner):

            @pl.when((z < n_inner - 1) & (src <= z))
            def _():
                gather_up(p, src).wait_send()

            @pl.when((z > 0) & (src >= z))
            def _():
                gather_dn(p, src).wait_send()

            gather_y(p, src).wait_send()
        for chunk in range(chunks):
            gather_sib(p, chunk).wait_send()
    for step in range(1, n_inner):
        sk_along(step).wait_send()
    sk_to_y.wait_send()
    sk_near.wait_send()
    sk_far.wait_send()
    for b in range(blocks):
        to_sib(b).wait_send()
        for dest in range(n_inner):
            reduce_y(b, dest).wait_send()
        for step in range(1, n_inner):
            reduce_z(b, step).wait_send()


def gather_plan(
    quant_rows, block_scales, expert_ids, gate_scores, w_gate, w_up, w_down, sketch, owner_map
):
    n_expert = lax.axis_size("expert")
    n_inner = lax.axis_size("inner")
    devices = n_expert * n_inner
    chunks = devices // 2
    tok, width = quant_rows.shape
    experts = owner_map.shape[0]
    half = width // 2
    rows2 = 2 * tok
    total = devices * tok
    units = w_gate.shape[2]
    share, cols = sketch.shape[1:]
    group = total // n_inner
    blocks = BLOCKS
    wide = half // blocks
    bf16, f32 = jnp.bfloat16, jnp.float32
    vmem = pl.BlockSpec(memory_space=pltpu.VMEM)
    hbm = pl.BlockSpec(memory_space=pl.ANY)
    dma = pltpu.SemaphoreType.DMA
    flops = 2 * total * (3 * width * units + share * cols) + 2 * experts * total * cols * cols
    return pl.pallas_call(
        functools.partial(layer_kernel, n_inner, experts),
        out_shape=(
            jax.ShapeDtypeStruct((tok, width), bf16),
            jax.ShapeDtypeStruct((1, cols, cols), f32),
        ),
        in_specs=[vmem] * 4 + [hbm] * 4 + [pl.BlockSpec(memory_space=pltpu.SMEM)],
        out_specs=(vmem, vmem),
        scratch_shapes=[
            pltpu.VMEM((width, units), bf16),
            pltpu.VMEM((width, units), bf16),
            pltpu.VMEM((units, width), bf16),
            pltpu.VMEM((share, cols), bf16),
            pltpu.VMEM((2, tok, half + LANES), f32),
            pltpu.VMEM((tok, half + LANES), f32),
            pltpu.VMEM((2, chunks, rows2, half // 2 + LANES), bf16),
            pltpu.VMEM((2, chunks, rows2, half // 2), bf16),
            pltpu.VMEM((total, units), f32),
            pltpu.VMEM((total, units), f32),
            pltpu.VMEM((n_inner, group, cols), bf16),
            pltpu.VMEM((n_inner, group, cols), bf16),
            pltpu.VMEM((devices, group, cols), bf16),
            pltpu.VMEM((total, units), bf16),
            pltpu.VMEM((blocks, chunks, rows2, wide), f32),
            pltpu.VMEM((blocks, chunks, rows2, wide), bf16),
            pltpu.VMEM((blocks, chunks, rows2, wide), bf16),
        ]
        + [pltpu.VMEM((blocks, n_inner, rows2, wide), bf16)] * 4
        + [
            pltpu.VMEM((2, blocks, tok, wide), f32),
            pltpu.VMEM((blocks, tok, wide), f32),
            dma((4,)),
            dma((2,)),
        ]
        + [dma((2, n_inner))] * 6
        + [dma((2, chunks))] * 2
        + [dma((n_inner,))] * 4
        + [dma((6,))]
        + [dma((blocks,))] * 2
        + [dma((blocks, n_inner))] * 4
        + [dma((2,))],
        cost_estimate=pl.CostEstimate(
            flops=flops,
            bytes_accessed=2 * (3 * width * units + share * cols),
            transcendentals=total * units,
        ),
        compiler_params=pltpu.CompilerParams(
            collective_id=0, has_side_effects=True, vmem_limit_bytes=56 * 1024 * 1024
        ),
    )(quant_rows, block_scales, expert_ids.T, gate_scores.T, w_gate, w_up, w_down, sketch, owner_map)


def per_device(
    quant_rows, block_scales, expert_ids, gate_scores, w_gate, w_up, w_down, sketch, owner_map
):
    small = lax.axis_size("expert") == 4 and lax.axis_size("inner") == 4
    plan = gather_plan if small else exchange_plan
    return plan(
        quant_rows, block_scales, expert_ids, gate_scores, w_gate, w_up, w_down, sketch, owner_map
    )


def solution(mesh):
    placed = (
        P(("groups", "expert", "inner"), None),
        P(("groups", "expert", "inner"), None),
        P(("groups", "expert", "inner"), None),
        P(("groups", "expert", "inner"), None),
        P("expert", None, "inner"),
        P("expert", None, "inner"),
        P("expert", "inner", None),
        P("expert", "inner", None),
        P(),
    )
    return jax.shard_map(
        per_device,
        mesh=mesh,
        in_specs=placed,
        out_specs=(
            P(("groups", "expert", "inner"), None),
            P(("groups", "expert", "inner"), None, None),
        ),
        check_vma=False,
    )
```
